32 devices in a mesh: groups: 2 (over y), tp: 16 (over z, x, core).
Axes of the slice: x: 2, y: 2, z: 4, core: 2. Of those that a mesh axis runs over, the one named last changes fastest.
Arguments:
- hidden: bfloat16 [16384, 8192], P(('groups', 'tp')), parts along dimension 0, may hold values from -8 to 8
- norm_gain: float32 [8192], replicated, may hold values from 0.1 to 1.9
- w_query: bfloat16 [8192, 4096], P('tp'), may hold values from -0.25 to 0.25
- b_query: float32 [4096], replicated, may hold values from -3 to 3
- w_key: bfloat16 [8192, 512], P('tp'), may hold values from -0.0677561 to 0.0677561
- w_value: bfloat16 [8192, 512], P('tp'), may hold values from -0.0625 to 0.0625
- b_value: float32 [512], replicated, may hold values from -4 to 4
- w_out: bfloat16 [4096, 8192], P('tp'), may hold values from -0.09375 to 0.09375
- step_ends: int32 [32], P('groups'), parts along dimension 0, may hold values from 0 to 8191, as said below
Outputs:
- scored_out: bfloat16 [32, 8192], P(('groups', 'tp')), parts along dimension 0
The draws below stay inside these ranges and needn't reach their ends.
There are 2 independent parts, one for each index of `groups`. The reference program is written for one: setup_inputs(seed, part) draws one part's arguments, and reference() takes and returns one part's arrays. A program takes and returns all parts, laid end to end along the dimension named above; an argument that names none is the same for every part. Nothing has to cross between parts.
Inputs may be any that keep to these rules, and one draw needn't show every extreme that they name: `step_ends`: entry i lies among tokens 512 * i to 512 * (i + 1) - 1; the last entry is the trace's last token.
All inputs are finite; a program needn't handle non-finite values.
Results may differ from the reference program's by a relative error of at most 0.012.
The reference program's roundings to bfloat16 on the way (of `normal_rows`, `key_rows`, `value_rows`, `scored_rows`, `queries`, `rounded_weights` and `attended`) count: a program that leaves them out, or rounds other values in their place, can miss the bound.
Values may be sent and summed in bfloat16 or wider, within the bound.
A program may use at most 128 MiB of HBM per device.

```python
import jax
import jax.numpy as jnp
from jax import lax

D = 8192
HEADS = 32
KV = 4
HEAD = 128
TOK_DEV = 512
TOKENS = 8192
SCORED = 16
N_TP = 16


def draw_hidden(key, part):
    key = jax.random.fold_in(key, 11)
    noise = jnp.clip(jax.random.normal(key, (TOKENS, D), jnp.float32), -6.0, 6.0)
    return noise.astype(jnp.bfloat16)


def draw_w_key(key, part):
    key = jax.random.fold_in(key, 12)
    matrix = jnp.clip(jax.random.normal(key, (D, KV * HEAD), jnp.float32), -6.0, 6.0)
    matrix = matrix.at[0, 0].set(6.0).at[1, 0].set(-6.0) * D ** (-0.5)
    return matrix.astype(jnp.bfloat16)


def draw_b_query(key, part):
    key = jax.random.fold_in(key, 13)
    values = jax.random.uniform(key, (HEADS * HEAD,), jnp.float32, -3.0, 3.0)
    return values.astype(jnp.float32)


def draw_step_ends(key, part):
    key = jax.random.fold_in(key, 14)
    offsets = jax.random.randint(key, (SCORED,), 0, TOK_DEV, dtype=jnp.int32)
    offsets = offsets.at[SCORED - 1].set(TOK_DEV - 1)
    return (jnp.arange(SCORED, dtype=jnp.int32) * TOK_DEV + offsets).astype(jnp.int32)


def spiked(values, stream_key, source, target, blocks, factor):
    def block_of(position):
        return (jnp.arange(values.shape[position]) // (values.shape[position] // blocks)).reshape((-1,) + (1,) * (values.ndim - 1 - position))

    first = jax.random.permutation(stream_key, blocks)[block_of(target)]
    second = (block_of(target) + blocks // 2) % blocks
    return jnp.where((block_of(source) == first) | (block_of(source) == second), factor * values, values)


def block_levels(own_key, shape, split, smallest, high):
    level, own = 1.0, jax.random.fold_in(own_key, 6)
    for position, shards_of in split:
        heights = jnp.exp(jax.random.uniform(jax.random.fold_in(own, position), (shards_of,), jnp.float32, smallest / len(split), high / len(split)))
        level = level * jnp.repeat(heights, shape[position] // shards_of).reshape([-1 if axis == position else 1 for axis in range(len(shape))])
    return level


def centred(own_key, extent, scale, limit, cuts=(), kind=jnp.bfloat16):
    gain = block_levels(own_key, extent, cuts, -0.22, 0.18) if cuts else 1.0
    values = jax.random.normal(own_key, extent, jnp.float32) * scale * gain
    return jnp.minimum(jnp.maximum(values, -limit), limit).astype(kind)


def bell_draw_with(key, shape, width, bound, cuts, heavy, held_as=jnp.bfloat16):
    result = width * jax.random.normal(key, shape, jnp.float32)
    if cuts:
        result = result * block_levels(key, shape, cuts, -0.22, 0.18)
    return jnp.clip(spiked(result, jax.random.fold_in(key, 3), *heavy), -bound, bound).astype(held_as)


def setup_inputs(seed: int = 0, part: int = 0) -> dict:
    keys = jax.random.split(jax.random.key(seed), 10)
    part_keys = jax.random.split(jax.random.fold_in(keys[9], part), 10)
    return {
        "hidden": draw_hidden(jax.random.fold_in(jax.random.fold_in(keys[9], part), 71), part),
        "norm_gain": jnp.clip(1.0 + 0.18 * jax.random.normal(keys[1], (D,), jnp.float32), 0.1, 1.9),
        "w_query": bell_draw_with(keys[2], (D, HEADS * HEAD), (D // 8) ** -0.5, 0.25, ((0, 16),), (0, 1, 16, 2.0)),
        "b_query": draw_b_query(jax.random.fold_in(keys[9], 71), part),
        "w_key": draw_w_key(jax.random.fold_in(keys[9], 71), part),
        "w_value": centred(keys[5], (D, KV * HEAD), D ** -0.5, 0.0625, ((0, 16),)),
        "b_value": centred(keys[6], (KV * HEAD,), 1.0, 4.0, (), jnp.float32),
        "w_out": centred(keys[7], (HEADS * HEAD, D), (HEADS * HEAD) ** -0.5, 0.09375, ((0, 16),)),
        "step_ends": draw_step_ends(jax.random.fold_in(jax.random.fold_in(keys[9], part), 71), part),
    }


def normed(rows, norm_gain):
    widened = rows.astype(jnp.float32)
    inverse_rms = lax.rsqrt(lax.optimization_barrier(jnp.mean(widened * widened, axis=-1, keepdims=True)) + 1e-06)
    return (widened * inverse_rms * norm_gain).astype(jnp.bfloat16)

def reference(hidden, norm_gain, w_query, b_query, w_key, w_value, b_value, w_out, step_ends):
    blocks = hidden.reshape(N_TP, TOK_DEV, D)

    def project(token_block):
        normal_rows = normed(token_block, norm_gain)
        key_rows = jnp.dot(normal_rows, w_key, preferred_element_type=jnp.float32).astype(jnp.bfloat16)
        value_rows = (jnp.dot(normal_rows, w_value, preferred_element_type=jnp.float32) + b_value).astype(jnp.bfloat16)
        return (key_rows, value_rows)
    key_rows, value_rows = lax.map(project, blocks)
    key_rows = key_rows.reshape(TOKENS, KV, HEAD).transpose(1, 0, 2)
    value_rows = value_rows.reshape(TOKENS, KV, HEAD).transpose(1, 0, 2)
    scored_rows = normed(hidden[step_ends.astype(jnp.int32)], norm_gain)
    queries = (jnp.dot(scored_rows, w_query, preferred_element_type=jnp.float32) + b_query).astype(jnp.bfloat16)
    group_ratio = HEADS // KV
    query_groups = queries.reshape(SCORED, KV, group_ratio, HEAD).transpose(1, 0, 2, 3)
    query_groups = query_groups.reshape(KV, SCORED * group_ratio, HEAD)
    positions = jnp.arange(TOKENS, dtype=jnp.int32)
    limits = jnp.repeat(step_ends.astype(jnp.int32), group_ratio)
    visible = positions[None, :] <= limits[:, None]

    def attend(triple):
        query_block, key_block, value_block = triple
        scores = jnp.dot(query_block, key_block.T, preferred_element_type=jnp.float32) * HEAD ** (-0.5)
        scores = jnp.where(visible, scores, -1e+30)
        row_max = lax.optimization_barrier(jnp.max(scores, axis=1, keepdims=True))
        weights = jnp.where(visible, jnp.exp(scores - row_max), 0.0)
        denominator = lax.optimization_barrier(jnp.sum(weights, axis=1, keepdims=True))
        rounded_weights = weights.astype(jnp.bfloat16)
        summed = jnp.dot(rounded_weights, value_block, preferred_element_type=jnp.float32)
        return summed / denominator
    attended = lax.map(attend, (query_groups, key_rows, value_rows))
    attended = attended.reshape(KV, SCORED, group_ratio, HEAD).transpose(1, 0, 2, 3)
    attended = attended.reshape(SCORED, HEADS * HEAD).astype(jnp.bfloat16)
    return jnp.dot(attended, w_out, preferred_element_type=jnp.float32).astype(jnp.bfloat16)
```

```python
import jax
import jax.numpy as jnp
from jax import lax
from jax.experimental import pallas as pl
from jax.experimental.pallas import tpu as pltpu
from jax.sharding import PartitionSpec as P

HEADS = 32
KV = 4
HEAD = 128
MESH = pl.DeviceIdType.MESH


def normed(rows, norm_gain):
    widened = rows.astype(jnp.float32)
    inverse_rms = lax.rsqrt(jnp.mean(widened * widened, axis=-1, keepdims=True) + 1e-06)
    return (widened * inverse_rms * norm_gain).astype(jnp.bfloat16)


def shards(hidden, norm_gain, w_query, b_query, w_key, w_value, b_value, w_out, step_ends):
    devices = lax.axis_size("tp")
    device_index = lax.axis_index("tp")
    tok_rows = hidden.shape[0]
    scored_count = step_ends.shape[0]
    per_owner = scored_count // devices
    group_ratio = HEADS // KV
    normal_rows = normed(hidden, norm_gain)
    key_sum = jnp.dot(
        normal_rows,
        lax.all_gather(w_key, "tp", axis=0, tiled=True),
        preferred_element_type=jnp.float32,
    )
    value_sum = jnp.dot(
        normal_rows,
        lax.all_gather(w_value, "tp", axis=0, tiled=True),
        preferred_element_type=jnp.float32,
    )
    key_rows = key_sum.astype(jnp.bfloat16)
    value_rows = (value_sum + b_value).astype(jnp.bfloat16)
    own_positions = lax.dynamic_slice_in_dim(step_ends, device_index * per_owner, per_owner, 0)
    own_offsets = own_positions - device_index * tok_rows
    own_scored = jnp.take(normal_rows, own_offsets, axis=0)
    scored_cols = lax.all_to_all(own_scored, "tp", split_axis=1, concat_axis=0, tiled=True)
    partial_query = jnp.dot(scored_cols, w_query, preferred_element_type=jnp.float32)
    queries = (lax.psum(partial_query, "tp") + b_query).astype(jnp.bfloat16)
    query_blocks = queries.reshape(scored_count, KV, group_ratio, HEAD)
    key_blocks = key_rows.reshape(tok_rows, KV, HEAD)
    value_blocks = value_rows.reshape(tok_rows, KV, HEAD)
    scores = jnp.einsum(
        "sgrd,tgd->sgrt", query_blocks, key_blocks, preferred_element_type=jnp.float32
    ) * HEAD ** (-0.5)
    key_positions = device_index * tok_rows + jnp.arange(tok_rows, dtype=jnp.int32)
    visible = key_positions[None, None, None, :] <= step_ends[:, None, None, None]
    scores = jnp.where(visible, scores, -1e30)
    local_peak = jnp.max(scores, axis=3)
    global_peak = lax.pmax(local_peak, "tp")
    weights = jnp.where(visible, jnp.exp(scores - global_peak[..., None]), 0.0)
    denominator = jnp.sum(weights, axis=3)
    summed = jnp.einsum(
        "sgrt,tgd->sgrd",
        weights.astype(jnp.bfloat16),
        value_blocks,
        preferred_element_type=jnp.float32,
    )
    owner_sum, owner_total = (
        lax.psum_scatter(
            summed.reshape(scored_count, HEADS * HEAD), "tp", scatter_dimension=0, tiled=True
        ),
        lax.psum_scatter(
            denominator.reshape(scored_count, HEADS), "tp", scatter_dimension=0, tiled=True
        ),
    )
    attended = owner_sum.reshape(per_owner, HEADS, HEAD) / owner_total[..., None]
    mixed_row = attended.reshape(per_owner, HEADS * HEAD).astype(jnp.bfloat16)
    mixed_cols = lax.all_to_all(mixed_row, "tp", split_axis=1, concat_axis=0, tiled=True)
    return lax.psum_scatter(
        jnp.dot(mixed_cols, w_out, preferred_element_type=jnp.float32),
        "tp",
        scatter_dimension=0,
        tiled=True,
    ).astype(jnp.bfloat16)


RING = 8
SPLIT = 176
NORM_ROWS = 32


def kernel(
    row_ref, ends_ref, gain_ref, bq_ref, bv_ref, hidden_ref, wq_hbm, wk_hbm, wv_hbm, wo_hbm,
    out_ref,
    normal, held, acc, wq, wo, row_send, row_recv, cols, pq_send, pq_recv, q_all,
    o_send, o_recv, l_send, l_recv, lmat, tmat, f_rows, f_send, f_recv,
    load_sem, ring_send, ring_recv, y_send, y_recv, core_send, core_recv,
    a2a_send, a2a_recv,
):
    n = 16
    me = lax.axis_index("tp")
    y = lax.axis_index("groups")
    core = me % 2
    chip = me // 2
    x = chip % 2
    z = chip // 2
    pos = z * (1 - x) + (RING - 1 - z) * x
    partner = chip * 2 + 1 - core
    block = wk_hbm.shape[0]
    ring_rows = pl.ds(pl.multiple_of(y * SPLIT, 16), block - SPLIT)
    y_rows = pl.ds(pl.multiple_of(y * (block - SPLIT), 16), SPLIT)
    w_hbm = (wk_hbm, wv_hbm)

    def chip_at(p):
        p = (p + 2 * RING) % RING
        far = p // (RING // 2)
        return (1 - far) * (2 * p) + far * (2 * RING - 1 - 2 * p)

    def origin(d, k, c):
        return chip_at(pos + (2 * d - 1) * k) * 2 + c

    def ring_copy(d, k, src=None):
        slot = origin(d, k, core)
        return pltpu.make_async_remote_copy(
            src_ref=held.at[d, slot, ring_rows] if src is None else src.at[ring_rows],
            dst_ref=held.at[d, slot, ring_rows],
            send_sem=ring_send.at[d, k],
            recv_sem=ring_recv.at[d, k],
            device_id={"tp": chip_at(pos + (1 - 2 * d)) * 2 + core},
            device_id_type=MESH,
        )

    def ring_arrival(d, k):
        slot = origin(d, k + 1, core)
        return pltpu.make_async_remote_copy(
            src_ref=held.at[d, slot, ring_rows],
            dst_ref=held.at[d, slot, ring_rows],
            send_sem=ring_send.at[d, k],
            recv_sem=ring_recv.at[d, k],
            device_id={"tp": chip_at(pos + (1 - 2 * d)) * 2 + core},
            device_id_type=MESH,
        )

    def y_copy(d, k, rows):
        slot = origin(d, k, core)
        return pltpu.make_async_remote_copy(
            src_ref=held.at[d, slot, rows],
            dst_ref=held.at[d, slot, rows],
            send_sem=y_send.at[d, k],
            recv_sem=y_recv.at[d, k],
            device_id={"groups": 1 - y},
            device_id_type=MESH,
        )

    peer_rows = pl.ds(pl.multiple_of((1 - y) * (block - SPLIT), 16), SPLIT)

    def core_copy(d, k, c, src=None):
        slot = origin(d, k, c)
        return pltpu.make_async_remote_copy(
            src_ref=held.at[d, slot] if src is None else src,
            dst_ref=held.at[d, slot],
            send_sem=core_send.at[d, k],
            recv_sem=core_recv.at[d, k],
            device_id={"tp": partner},
            device_id_type=MESH,
        )

    def peer_copy(phase, peer, slot, send, recv):
        return pltpu.make_async_remote_copy(
            src_ref=send,
            dst_ref=recv.at[slot],
            send_sem=a2a_send.at[phase, peer],
            recv_sem=a2a_recv.at[phase, slot],
            device_id={"tp": peer},
            device_id_type=MESH,
        )

    def for_peers(body):
        @pl.loop(1, n)
        def _(k):
            body((me + k) % n)

    def exchange(phase, send_of, recv):
        for_peers(lambda peer: peer_copy(phase, peer, me, send_of(peer), recv).start())

    def arrive(phase, send_of, recv):
        for_peers(lambda peer: peer_copy(phase, peer, peer, send_of(peer), recv).wait_recv())

    def sent(phase, send_of, recv):
        for_peers(lambda peer: peer_copy(phase, peer, me, send_of(peer), recv).wait_send())

    loads = [
        pltpu.make_async_copy(hidden_ref, normal, load_sem.at[0]),
        pltpu.make_async_copy(wq_hbm, wq, load_sem.at[1]),
        pltpu.make_async_copy(wk_hbm, held.at[0, me], load_sem.at[2]),
        pltpu.make_async_copy(wv_hbm, held.at[1, me], load_sem.at[3]),
        pltpu.make_async_copy(wo_hbm, wo, load_sem.at[4]),
    ]
    for load in loads:
        load.start()

    barrier = pltpu.get_barrier_semaphore()
    for_peers(
        lambda peer: pl.semaphore_signal(
            barrier, inc=1, device_id={"tp": peer}, device_id_type=MESH
        )
    )
    pl.semaphore_signal(barrier, inc=1, device_id={"groups": 1 - y}, device_id_type=MESH)
    pl.semaphore_wait(barrier, n)

    for d in range(2):
        ring_copy(d, 0, w_hbm[d]).start()
    for d in range(2):
        core_copy(d, 0, core, w_hbm[d]).start()

    row = row_ref[...]
    row_scale = lax.rsqrt(jnp.sum(row * row, axis=-1, keepdims=True) / row.shape[1] + 1e-06)
    for j in range(n):
        part = pl.ds(j * block, block)
        piece = row_ref[:, part] * row_scale * gain_ref[:, part]
        row_send[j] = piece.astype(jnp.bfloat16).astype(jnp.float32)
    row_recv[pl.ds(me, 1)] = row_send[pl.ds(me, 1)]
    row_of = lambda peer: row_send.at[peer]
    exchange(0, row_of, row_recv)
    for load in loads:
        load.wait()

    width = normal.shape[1]
    piece_lanes = 256

    def norm_rows(first, last):
        @pl.loop(first, last)
        def _(i):
            rows = pl.ds(pl.multiple_of(i * NORM_ROWS, NORM_ROWS), NORM_ROWS)
            squares = jnp.zeros((NORM_ROWS, piece_lanes), jnp.float32)
            for c in range(0, width, piece_lanes):
                v = normal[rows, pl.ds(c, piece_lanes)].astype(jnp.float32)
                squares = squares + v * v
            scale = lax.rsqrt(jnp.sum(squares, axis=-1, keepdims=True) / width + 1e-06)
            for c in range(0, width, piece_lanes):
                lanes = pl.ds(c, piece_lanes)
                v = normal[rows, lanes].astype(jnp.float32)
                normal[rows, lanes] = (v * scale * gain_ref[:, lanes]).astype(jnp.bfloat16)

    tok_rows = normal.shape[0]
    steps = tok_rows // NORM_ROWS
    norm_rows(0, steps // 2)
    acc[...] = jnp.zeros_like(acc)

    def project(k, c):
        @pl.loop(0, 2)
        def _(d):
            slot = origin(d, k, c)
            lanes = pl.ds(pl.multiple_of(slot * block, block), block)
            acc[d] += jnp.dot(
                normal[:, lanes], held[d, slot], preferred_element_type=jnp.float32
            )

    share = wq.shape[1] // n
    pq_of = lambda peer: pq_send.at[peer]
    q_of = lambda peer: q_all.at[me]

    @pl.loop(0, RING - 1)
    def _(s):
        for d in range(2):
            ring_arrival(d, s).wait_recv()

            @pl.when(s < RING - 2)
            def _():
                ring_copy(d, s + 1).start()

            y_copy(d, s + 1, y_rows).start()

        @pl.when(s >= 1)
        def _():
            for d in range(2):
                y_copy(d, s, peer_rows).wait_recv()
                core_copy(d, s, core).start()

        @pl.when(s == 0)
        def _():
            arrive(0, row_of, row_recv)
            for j in range(n):
                cols[j : j + 1, :] = row_recv[j]
            scored = cols[...].astype(jnp.bfloat16)

            @pl.loop(0, n)
            def _(j):
                pq_send[j] = jnp.dot(
                    scored,
                    wq[:, pl.ds(pl.multiple_of(j * share, share), share)],
                    preferred_element_type=jnp.float32,
                )

            pq_recv[pl.ds(me, 1)] = pq_send[pl.ds(me, 1)]
            exchange(1, pq_of, pq_recv)
            norm_rows(steps // 2, steps)
            project(0, core)

        @pl.when(s == 1)
        def _():
            arrive(1, pq_of, pq_recv)
            total = pq_recv[0]
            for j in range(1, n):
                total = total + pq_recv[j]
            bias = bq_ref[:, pl.ds(pl.multiple_of(me * share, share), share)]
            q_all[me] = (total + bias).astype(jnp.bfloat16)
            exchange(2, q_of, q_all)

        @pl.when(s >= 1)
        def _():
            project(s, core)
            for d in range(2):
                core_copy(d, s - 1, 1 - core).wait_recv()
            project(s - 1, 1 - core)

    for d in range(2):
        y_copy(d, RING - 1, peer_rows).wait_recv()
        core_copy(d, RING - 1, core).start()
    project(RING - 1, core)
    for k in (RING - 2, RING - 1):
        for d in range(2):
            core_copy(d, k, 1 - core).wait_recv()
        project(k, 1 - core)

    arrive(2, q_of, q_all)
    key_rows = acc[0].astype(jnp.bfloat16)
    value_rows = (acc[1] + bv_ref[...]).astype(jnp.bfloat16)
    scored_count = n
    group_rows = scored_count * (HEADS // KV)
    per_group = n // KV
    row_of_score = lax.broadcasted_iota(jnp.int32, (group_rows, 1), 0) % scored_count
    limit = jnp.zeros((group_rows, 1), jnp.int32)
    for j in range(scored_count):
        limit = jnp.where(row_of_score == j, ends_ref[j], limit)
    token = lax.broadcasted_iota(jnp.int32, (group_rows, tok_rows), 1) + me * tok_rows
    visible = token <= limit
    own_rows = group_rows // per_group

    for g in range(KV):
        heads = slice(g * HEAD, (g + 1) * HEAD)
        query = jnp.concatenate(
            [
                q_all[g * per_group + j][:, h * HEAD : (h + 1) * HEAD]
                for j in range(per_group)
                for h in range(share // HEAD)
            ],
            axis=0,
        )
        scores = lax.dot_general(
            query,
            key_rows[:, heads],
            (((1,), (1,)), ((), ())),
            preferred_element_type=jnp.float32,
        ) * HEAD ** (-0.5)
        scores = jnp.where(visible, scores, -1e30)
        peak = jnp.max(scores, axis=1, keepdims=True)
        weights = jnp.where(visible, jnp.exp(scores - peak), 0.0)
        total = jnp.sum(weights, axis=1, keepdims=True)
        summed = jnp.dot(
            weights.astype(jnp.bfloat16), value_rows[:, heads], preferred_element_type=jnp.float32
        )
        some = total > 0.0
        total = jnp.where(some, total, 1.0)
        level = jnp.where(some, peak + jnp.log(total), -1e30)
        l_send[g] = jnp.transpose(jnp.broadcast_to(level, (group_rows, HEAD)))[0:8, :]
        part = (summed / total).astype(jnp.bfloat16)
        for j in range(per_group):
            dest = g * per_group + j
            o_send[dest] = part[j * own_rows : (j + 1) * own_rows, :]

            @pl.when(me != dest)
            def _():
                peer_copy(3, dest, me, o_send.at[dest], o_recv).start()
                peer_copy(4, dest, me, l_send.at[g], l_recv).start()

    o_of = lambda peer: o_send.at[peer]
    l_of = lambda peer: l_send.at[peer // per_group]
    o_recv[me] = o_send[me]
    l_recv[me] = l_send[me // per_group]
    arrive(4, l_of, l_recv)
    lmat[...] = jnp.zeros_like(lmat)
    for j in range(n):
        lmat[j : j + 1, :] = l_recv[j][0:1, :]
    levels = lmat[0:n, :]
    mass = jnp.exp(levels - jnp.max(levels, axis=0, keepdims=True))
    lmat[0:n, :] = mass / jnp.sum(mass, axis=0, keepdims=True)
    tmat[...] = jnp.transpose(lmat[...])
    factor = tmat[pl.ds(pl.multiple_of((me % per_group) * own_rows, own_rows), own_rows), :]
    arrive(3, o_of, o_recv)
    attended = jnp.zeros((own_rows, HEAD), jnp.float32)
    for j in range(n):
        attended = attended + factor[:, j : j + 1] * o_recv[j].astype(jnp.float32)
    mixed = jnp.concatenate(
        [attended[0:scored_count], attended[scored_count:own_rows]], axis=1
    ).astype(jnp.bfloat16)

    chunk_lanes = wo.shape[1] // n
    for c in range(n):
        chunk = jnp.dot(
            mixed, wo[:, pl.ds(c * chunk_lanes, chunk_lanes)], preferred_element_type=jnp.float32
        )
        for j in range(n):
            f_rows[j, c : c + 1, :] = chunk[j : j + 1, :]
    f_of = lambda peer: f_send.at[peer]

    @pl.loop(0, n)
    def _(j):
        f_send[j] = f_rows[j].astype(jnp.bfloat16)

    exchange(5, f_of, f_recv)
    f_recv[me] = f_send[me]
    sent(0, row_of, row_recv)
    sent(1, pq_of, pq_recv)
    sent(2, q_of, q_all)
    sent(3, o_of, o_recv)
    sent(4, l_of, l_recv)
    for d in range(2):
        ring_copy(d, 0, w_hbm[d]).wait_send()
        core_copy(d, 0, core, w_hbm[d]).wait_send()

        @pl.loop(1, RING)
        def _(k):
            @pl.when(k < RING - 1)
            def _():
                ring_copy(d, k).wait_send()

            y_copy(d, k, y_rows).wait_send()
            core_copy(d, k, core).wait_send()

    arrive(5, f_of, f_recv)
    result = f_recv[0].astype(jnp.float32)
    for j in range(1, n):
        result = result + f_recv[j].astype(jnp.float32)
    out_ref[...] = result.astype(jnp.bfloat16)
    sent(5, f_of, f_recv)


def fused(hidden, norm_gain, w_query, b_query, w_key, w_value, b_value, w_out, step_ends):
    n = lax.axis_size("tp")
    me = lax.axis_index("tp")
    tok_rows, width = hidden.shape
    offset = lax.dynamic_slice_in_dim(step_ends, me, 1, 0)[0] - me * tok_rows
    own_row = lax.dynamic_slice_in_dim(hidden, offset, 1, 0).astype(jnp.float32)
    block, kv_cols = w_key.shape
    share = w_query.shape[1] // n
    chunk = w_out.shape[1] // n
    bf16, f32 = jnp.bfloat16, jnp.float32
    vmem = pl.BlockSpec(memory_space=pltpu.VMEM)
    far = pl.BlockSpec(memory_space=pl.ANY)
    dma = pltpu.SemaphoreType.DMA
    own_rows = n * (share // HEAD)
    out = pl.pallas_call(
        kernel,
        out_shape=jax.ShapeDtypeStruct((n, chunk), bf16),
        in_specs=[vmem, pl.BlockSpec(memory_space=pltpu.SMEM), vmem, vmem, vmem] + [far] * 5,
        out_specs=vmem,
        scratch_shapes=[
            pltpu.VMEM((tok_rows, width), bf16),
            pltpu.VMEM((2, n, block, kv_cols), bf16),
            pltpu.VMEM((2, tok_rows, kv_cols), f32),
            pltpu.VMEM(w_query.shape, bf16),
            pltpu.VMEM(w_out.shape, bf16),
            pltpu.VMEM((n, 1, block), f32),
            pltpu.VMEM((n, 1, block), f32),
            pltpu.VMEM((n, block), f32),
            pltpu.VMEM((n, n, share), f32),
            pltpu.VMEM((n, n, share), f32),
            pltpu.VMEM((n, n, share), bf16),
            pltpu.VMEM((n, own_rows, HEAD), bf16),
            pltpu.VMEM((n, own_rows, HEAD), bf16),
            pltpu.VMEM((KV, 8, HEAD), f32),
            pltpu.VMEM((n, 8, HEAD), f32),
            pltpu.VMEM((HEAD, HEAD), f32),
            pltpu.VMEM((HEAD, HEAD), f32),
            pltpu.VMEM((n, n, chunk), f32),
            pltpu.VMEM((n, n, chunk), bf16),
            pltpu.VMEM((n, n, chunk), bf16),
            dma((5,)),
            dma((2, RING)),
            dma((2, RING)),
            dma((2, RING)),
            dma((2, RING)),
            dma((2, RING)),
            dma((2, RING)),
            dma((6, n)),
            dma((6, n)),
        ],
        compiler_params=pltpu.CompilerParams(
            collective_id=0, has_side_effects=True, vmem_limit_bytes=54 * 2**20
        ),
    )(
        own_row,
        step_ends,
        norm_gain.reshape(1, -1),
        b_query.reshape(1, -1),
        b_value.reshape(1, -1),
        hidden,
        w_query,
        w_key,
        w_value,
        w_out,
    )
    return out.reshape(1, n * chunk)


def solution(mesh):
    in_specs = (
        P(("groups", "tp"), None),
        P(),
        P("tp", None),
        P(),
        P("tp", None),
        P("tp", None),
        P(),
        P("tp", None),
        P("groups"),
    )
    out_specs = P(("groups", "tp"), None)
    small = (mesh.shape["groups"], mesh.shape["tp"]) == (2, 16)
    return jax.shard_map(
        fused if small else shards,
        mesh=mesh,
        in_specs=in_specs,
        out_specs=out_specs,
        check_vma=False,
    )
```

```python
import jax
import jax.numpy as jnp
from jax import lax
from jax.experimental import pallas as pl
from jax.experimental.pallas import tpu as pltpu
from jax.sharding import PartitionSpec as P

HEADS = 32
KV = 4
HEAD = 128
MESH = pl.DeviceIdType.MESH


def normed(rows, norm_gain):
    widened = rows.astype(jnp.float32)
    inverse_rms = lax.rsqrt(jnp.mean(widened * widened, axis=-1, keepdims=True) + 1e-06)
    return (widened * inverse_rms * norm_gain).astype(jnp.bfloat16)


def shards(hidden, norm_gain, w_query, b_query, w_key, w_value, b_value, w_out, step_ends):
    devices = lax.axis_size("tp")
    device_index = lax.axis_index("tp")
    tok_rows = hidden.shape[0]
    scored_count = step_ends.shape[0]
    per_owner = scored_count // devices
    group_ratio = HEADS // KV
    normal_rows = normed(hidden, norm_gain)
    key_sum = jnp.dot(
        normal_rows,
        lax.all_gather(w_key, "tp", axis=0, tiled=True),
        preferred_element_type=jnp.float32,
    )
    value_sum = jnp.dot(
        normal_rows,
        lax.all_gather(w_value, "tp", axis=0, tiled=True),
        preferred_element_type=jnp.float32,
    )
    key_rows = key_sum.astype(jnp.bfloat16)
    value_rows = (value_sum + b_value).astype(jnp.bfloat16)
    own_positions = lax.dynamic_slice_in_dim(step_ends, device_index * per_owner, per_owner, 0)
    own_offsets = own_positions - device_index * tok_rows
    own_scored = jnp.take(normal_rows, own_offsets, axis=0)
    scored_cols = lax.all_to_all(own_scored, "tp", split_axis=1, concat_axis=0, tiled=True)
    partial_query = jnp.dot(scored_cols, w_query, preferred_element_type=jnp.float32)
    queries = (lax.psum(partial_query, "tp") + b_query).astype(jnp.bfloat16)
    query_blocks = queries.reshape(scored_count, KV, group_ratio, HEAD)
    key_blocks = key_rows.reshape(tok_rows, KV, HEAD)
    value_blocks = value_rows.reshape(tok_rows, KV, HEAD)
    scores = jnp.einsum(
        "sgrd,tgd->sgrt", query_blocks, key_blocks, preferred_element_type=jnp.float32
    ) * HEAD ** (-0.5)
    key_positions = device_index * tok_rows + jnp.arange(tok_rows, dtype=jnp.int32)
    visible = key_positions[None, None, None, :] <= step_ends[:, None, None, None]
    scores = jnp.where(visible, scores, -1e30)
    local_peak = jnp.max(scores, axis=3)
    global_peak = lax.pmax(local_peak, "tp")
    weights = jnp.where(visible, jnp.exp(scores - global_peak[..., None]), 0.0)
    denominator = jnp.sum(weights, axis=3)
    summed = jnp.einsum(
        "sgrt,tgd->sgrd",
        weights.astype(jnp.bfloat16),
        value_blocks,
        preferred_element_type=jnp.float32,
    )
    owner_sum, owner_total = (
        lax.psum_scatter(
            summed.reshape(scored_count, HEADS * HEAD), "tp", scatter_dimension=0, tiled=True
        ),
        lax.psum_scatter(
            denominator.reshape(scored_count, HEADS), "tp", scatter_dimension=0, tiled=True
        ),
    )
    attended = owner_sum.reshape(per_owner, HEADS, HEAD) / owner_total[..., None]
    mixed_row = attended.reshape(per_owner, HEADS * HEAD).astype(jnp.bfloat16)
    mixed_cols = lax.all_to_all(mixed_row, "tp", split_axis=1, concat_axis=0, tiled=True)
    return lax.psum_scatter(
        jnp.dot(mixed_cols, w_out, preferred_element_type=jnp.float32),
        "tp",
        scatter_dimension=0,
        tiled=True,
    ).astype(jnp.bfloat16)


RING = 8
SPLIT = 176
LAST = 64
NORM_ROWS = 32


def kernel(
    ends_ref, gain_ref, bq_ref, bv_ref, hidden_ref, wq_hbm, wk_hbm, wv_hbm, wo_hbm,
    out_ref,
    normal, own_row, held, acc, wq, wo, row_send, row_recv, cols, pq_send, pq_pair, pq_recv, q_all,
    o_send, o_recv, l_send, l_recv, lmat, tmat, f_rows, f_send, f_recv,
    load_sem, ring_send, ring_recv, y_send, y_recv, core_send, core_recv,
    a2a_send, a2a_recv, pair_send, pair_recv,
):
    n = 16
    me = lax.axis_index("tp")
    y = lax.axis_index("groups")
    core = me % 2
    chip = me // 2
    x = chip % 2
    z = chip // 2
    pos = z * (1 - x) + (RING - 1 - z) * x
    partner = chip * 2 + 1 - core
    block = wk_hbm.shape[0]
    w_hbm = (wk_hbm, wv_hbm)

    def chip_at(p):
        p = (p + 2 * RING) % RING
        far = p // (RING // 2)
        return (1 - far) * (2 * p) + far * (2 * RING - 1 - 2 * p)

    def origin(d, k, c):
        return chip_at(pos + (2 * d - 1) * k) * 2 + c

    def rows_of(part):
        if part == 0:
            return pl.ds(pl.multiple_of(y * (block - SPLIT), 16), SPLIT)
        if part == 1:
            return pl.ds(SPLIT, block - 2 * SPLIT)
        return pl.ds(pl.multiple_of((1 - y) * (block - SPLIT) + LAST, 16), SPLIT - LAST)

    def ring_part(d, k, part, slot, src):
        return pltpu.make_async_remote_copy(
            src_ref=(held.at[d, slot] if src is None else src).at[rows_of(part)],
            dst_ref=held.at[d, slot, rows_of(part)],
            send_sem=ring_send.at[part, d, k],
            recv_sem=ring_recv.at[part, d, k],
            device_id={"tp": chip_at(pos + (1 - 2 * d)) * 2 + core},
            device_id_type=MESH,
        )

    def ring_copy(d, k, part, src=None):
        return ring_part(d, k, part, origin(d, k, core), src)

    def ring_arrival(d, k, part):
        return ring_part(d, k, part, origin(d, k + 1, core), None)

    def y_copy(d, k, owner, count=SPLIT):
        slot = origin(d, k, core)
        rows = pl.ds(pl.multiple_of(owner * (block - SPLIT), 16), count)
        return pltpu.make_async_remote_copy(
            src_ref=held.at[d, slot, rows],
            dst_ref=held.at[d, slot, rows],
            send_sem=y_send.at[d, k],
            recv_sem=y_recv.at[d, k],
            device_id={"groups": 1 - y},
            device_id_type=MESH,
        )

    def core_copy(d, k, c, src=None):
        slot = origin(d, k, c)
        return pltpu.make_async_remote_copy(
            src_ref=held.at[d, slot] if src is None else src,
            dst_ref=held.at[d, slot],
            send_sem=core_send.at[d, k],
            recv_sem=core_recv.at[d, k],
            device_id={"tp": partner},
            device_id_type=MESH,
        )

    def peer_copy(phase, peer, slot, send, recv):
        return pltpu.make_async_remote_copy(
            src_ref=send,
            dst_ref=recv.at[slot],
            send_sem=a2a_send.at[phase, peer],
            recv_sem=a2a_recv.at[phase, slot],
            device_id={"tp": peer},
            device_id_type=MESH,
        )

    def for_peers(body):
        @pl.loop(1, n)
        def _(k):
            body((me + k) % n)

    def exchange(phase, send_of, recv):
        for_peers(lambda peer: peer_copy(phase, peer, me, send_of(peer), recv).start())

    def arrive(phase, send_of, recv):
        for_peers(lambda peer: peer_copy(phase, peer, peer, send_of(peer), recv).wait_recv())

    def sent(phase, send_of, recv):
        for_peers(lambda peer: peer_copy(phase, peer, me, send_of(peer), recv).wait_send())

    loads = [
        pltpu.make_async_copy(hidden_ref, normal, load_sem.at[0]),
        pltpu.make_async_copy(wq_hbm, wq, load_sem.at[1]),
        pltpu.make_async_copy(wk_hbm, held.at[0, me], load_sem.at[2]),
        pltpu.make_async_copy(wv_hbm, held.at[1, me], load_sem.at[3]),
        pltpu.make_async_copy(wo_hbm, wo, load_sem.at[4]),
    ]
    for load in loads:
        load.start()

    barrier = pltpu.get_barrier_semaphore()
    for_peers(
        lambda peer: pl.semaphore_signal(
            barrier, inc=1, device_id={"tp": peer}, device_id_type=MESH
        )
    )
    pl.semaphore_signal(barrier, inc=1, device_id={"groups": 1 - y}, device_id_type=MESH)
    pl.semaphore_wait(barrier, n)

    for part in range(2):
        for d in range(2):
            ring_copy(d, 0, part, w_hbm[d]).start()
    for d in range(2):
        core_copy(d, 0, core, w_hbm[d]).start()

    row_of = lambda peer: row_send.at[peer]
    tok_rows = normal.shape[0]
    offset = ends_ref[me] % tok_rows
    width = normal.shape[1]
    piece_lanes = 256

    def norm_rows(first, last):
        @pl.loop(first, last)
        def _(i):
            rows = pl.ds(pl.multiple_of(i * NORM_ROWS, NORM_ROWS), NORM_ROWS)
            picked = i * NORM_ROWS + lax.broadcasted_iota(jnp.int32, (NORM_ROWS, 1), 0) == offset
            squares = jnp.zeros((NORM_ROWS, piece_lanes), jnp.float32)
            for c in range(0, width, piece_lanes):
                v = normal[rows, pl.ds(c, piece_lanes)].astype(jnp.float32)
                squares = squares + v * v
            scale = lax.rsqrt(jnp.sum(squares, axis=-1, keepdims=True) / width + 1e-06)
            for c in range(0, width, piece_lanes):
                lanes = pl.ds(c, piece_lanes)
                v = normal[rows, lanes].astype(jnp.float32)
                rounded = (v * scale * gain_ref[:, lanes]).astype(jnp.bfloat16)
                normal[rows, lanes] = rounded
                own = jnp.where(picked, rounded.astype(jnp.float32), 0.0)
                own_row[:, lanes] += own[0:8] + own[8:16] + own[16:24] + own[24:32]

    steps = tok_rows // NORM_ROWS

    def project(k, c):
        @pl.loop(0, 2)
        def _(d):
            slot = origin(d, k, c)
            lanes = pl.ds(pl.multiple_of(slot * block, block), block)
            acc[d] += jnp.dot(
                normal[:, lanes], held[d, slot], preferred_element_type=jnp.float32
            )

    share = wq.shape[1] // n

    def chip_copy(phase, other, slot, send, recv):
        return pltpu.make_async_remote_copy(
            src_ref=send,
            dst_ref=recv.at[slot],
            send_sem=a2a_send.at[phase, other],
            recv_sem=a2a_recv.at[phase, slot],
            device_id={"tp": other * 2 + core},
            device_id_type=MESH,
        )

    def for_chips(body):
        @pl.loop(1, RING)
        def _(k):
            body((chip + k) % RING)

    def pair_copy(phase, send, recv):
        return pltpu.make_async_remote_copy(
            src_ref=send,
            dst_ref=recv,
            send_sem=pair_send.at[phase],
            recv_sem=pair_recv.at[phase],
            device_id={"tp": partner},
            device_id_type=MESH,
        )

    pq_of = lambda other: pq_send.at[core, other]
    q_of = lambda other: q_all.at[core, chip]
    pq_swap = lambda: pair_copy(0, pq_send.at[1 - core], pq_pair)
    q_swap = lambda c: pair_copy(1, q_all.at[c], q_all.at[c])

    @pl.loop(0, RING - 2)
    def _(s):
        for part in range(2):
            for d in range(2):
                ring_arrival(d, s, part).wait_recv()
                ring_copy(d, s + 1, part).start()
                if part == 0:
                    y_copy(d, s + 1, y).start()

        @pl.when(s >= 1)
        def _():
            for d in range(2):
                y_copy(d, s, 1 - y).wait_recv()
                core_copy(d, s, core).start()

        @pl.when(s == 0)
        def _():
            acc[...] = jnp.zeros_like(acc)
            own_row[...] = jnp.zeros_like(own_row)
            for load in loads:
                load.wait()
            norm_rows(0, steps)
            for j in range(n):
                row_send[j] = jnp.sum(own_row[:, pl.ds(j * block, block)], axis=0, keepdims=True)
            row_recv[pl.ds(me, 1)] = row_send[pl.ds(me, 1)]
            exchange(0, row_of, row_recv)
            project(0, core)

        @pl.when(s == 1)
        def _():
            arrive(0, row_of, row_recv)
            for j in range(n):
                cols[j : j + 1, :] = row_recv[j]
            scored = cols[...].astype(jnp.bfloat16)

            @pl.loop(0, n)
            def _(j):
                pq_send[j % 2, j // 2] = jnp.dot(
                    scored,
                    wq[:, pl.ds(pl.multiple_of(j * share, share), share)],
                    preferred_element_type=jnp.float32,
                )

            pq_swap().start()

        @pl.when(s == 2)
        def _():
            pq_swap().wait_recv()
            pq_send[core] = pq_send[core] + pq_pair[...]
            for_chips(lambda other: chip_copy(1, other, chip, pq_of(other), pq_recv).start())
            pq_recv[chip] = pq_send[core, chip]

        @pl.when(s == 3)
        def _():
            for_chips(lambda other: chip_copy(1, other, other, pq_of(other), pq_recv).wait_recv())
            total = pq_recv[0]
            for j in range(1, RING):
                total = total + pq_recv[j]
            bias = bq_ref[:, pl.ds(pl.multiple_of(me * share, share), share)]
            q_all[core, chip] = (total + bias).astype(jnp.bfloat16)
            for_chips(lambda other: chip_copy(2, other, chip, q_of(other), q_all.at[core]).start())

        @pl.when(s == 4)
        def _():
            for_chips(
                lambda other: chip_copy(2, other, other, q_of(other), q_all.at[core]).wait_recv()
            )
            q_swap(core).start()

        @pl.when(s >= 1)
        def _():
            project(s, core)
            for d in range(2):
                core_copy(d, s - 1, 1 - core).wait_recv()
            project(s - 1, 1 - core)

    last = RING - 1
    for d in range(2):
        ring_arrival(d, last - 1, 0).wait_recv()
        y_copy(d, last, y, LAST).start()
    for d in range(2):
        y_copy(d, last - 1, 1 - y).wait_recv()
        ring_copy(d, last - 1, 2).start()
        core_copy(d, last - 1, core).start()
    project(last - 1, core)
    for d in range(2):
        core_copy(d, last - 2, 1 - core).wait_recv()
    project(last - 2, 1 - core)
    for d in range(2):
        ring_arrival(d, last - 1, 1).wait_recv()
        y_copy(d, last, 1 - y, LAST).wait_recv()
        ring_arrival(d, last - 1, 2).wait_recv()
        core_copy(d, last, core).start()
    for d in range(2):
        core_copy(d, last - 1, 1 - core).wait_recv()
    project(last - 1, 1 - core)
    project(last, core)
    for d in range(2):
        core_copy(d, last, 1 - core).wait_recv()
    project(last, 1 - core)
    q_swap(1 - core).wait_recv()

    key_rows = acc[0].astype(jnp.bfloat16)
    value_rows = (acc[1] + bv_ref[...]).astype(jnp.bfloat16)
    scored_count = n
    group_rows = scored_count * (HEADS // KV)
    per_group = n // KV
    row_of_score = lax.broadcasted_iota(jnp.int32, (group_rows, 1), 0) % scored_count
    limit = jnp.zeros((group_rows, 1), jnp.int32)
    for j in range(scored_count):
        limit = jnp.where(row_of_score == j, ends_ref[j], limit)
    token = lax.broadcasted_iota(jnp.int32, (group_rows, tok_rows), 1) + me * tok_rows
    visible = token <= limit
    own_rows = group_rows // per_group

    for g in range(KV):
        heads = slice(g * HEAD, (g + 1) * HEAD)
        query = jnp.concatenate(
            [
                q_all[(g * per_group + j) % 2, (g * per_group + j) // 2][:, h * HEAD : (h + 1) * HEAD]
                for j in range(per_group)
                for h in range(share // HEAD)
            ],
            axis=0,
        )
        scores = lax.dot_general(
            query,
            key_rows[:, heads],
            (((1,), (1,)), ((), ())),
            preferred_element_type=jnp.float32,
        ) * HEAD ** (-0.5)
        scores = jnp.where(visible, scores, -1e30)
        peak = jnp.max(scores, axis=1, keepdims=True)
        weights = jnp.where(visible, jnp.exp(scores - peak), 0.0)
        total = jnp.sum(weights, axis=1, keepdims=True)
        summed = jnp.dot(
            weights.astype(jnp.bfloat16), value_rows[:, heads], preferred_element_type=jnp.float32
        )
        some = total > 0.0
        total = jnp.where(some, total, 1.0)
        level = jnp.where(some, peak + jnp.log(total), -1e30)
        l_send[g] = jnp.transpose(jnp.broadcast_to(level, (group_rows, HEAD)))[0:8, :]
        part = (summed / total).astype(jnp.bfloat16)
        for j in range(per_group):
            dest = g * per_group + j
            o_send[dest] = part[j * own_rows : (j + 1) * own_rows, :]

            @pl.when(me != dest)
            def _():
                peer_copy(3, dest, me, o_send.at[dest], o_recv).start()
                peer_copy(4, dest, me, l_send.at[g], l_recv).start()

    o_of = lambda peer: o_send.at[peer]
    l_of = lambda peer: l_send.at[peer // per_group]
    o_recv[me] = o_send[me]
    l_recv[me] = l_send[me // per_group]
    arrive(4, l_of, l_recv)
    lmat[...] = jnp.zeros_like(lmat)
    for j in range(n):
        lmat[j : j + 1, :] = l_recv[j][0:1, :]
    levels = lmat[0:n, :]
    mass = jnp.exp(levels - jnp.max(levels, axis=0, keepdims=True))
    lmat[0:n, :] = mass / jnp.sum(mass, axis=0, keepdims=True)
    tmat[...] = jnp.transpose(lmat[...])
    factor = tmat[pl.ds(pl.multiple_of((me % per_group) * own_rows, own_rows), own_rows), :]
    arrive(3, o_of, o_recv)
    attended = jnp.zeros((own_rows, HEAD), jnp.float32)
    for j in range(n):
        attended = attended + factor[:, j : j + 1] * o_recv[j].astype(jnp.float32)
    mixed = jnp.concatenate(
        [attended[0:scored_count], attended[scored_count:own_rows]], axis=1
    ).astype(jnp.bfloat16)

    chunk_lanes = wo.shape[1] // n
    for c in range(n):
        chunk = jnp.dot(
            mixed, wo[:, pl.ds(c * chunk_lanes, chunk_lanes)], preferred_element_type=jnp.float32
        )
        for j in range(n):
            f_rows[j, c : c + 1, :] = chunk[j : j + 1, :]
    f_of = lambda peer: f_send.at[peer]

    @pl.loop(0, n)
    def _(j):
        f_send[j] = f_rows[j].astype(jnp.bfloat16)

    exchange(5, f_of, f_recv)
    f_recv[me] = f_send[me]
    sent(0, row_of, row_recv)
    for_chips(lambda other: chip_copy(1, other, chip, pq_of(other), pq_recv).wait_send())
    for_chips(lambda other: chip_copy(2, other, chip, q_of(other), q_all.at[core]).wait_send())
    pq_swap().wait_send()
    q_swap(core).wait_send()
    sent(3, o_of, o_recv)
    sent(4, l_of, l_recv)
    for d in range(2):
        for part in range(2):
            ring_copy(d, 0, part, w_hbm[d]).wait_send()
        core_copy(d, 0, core, w_hbm[d]).wait_send()

        @pl.loop(1, RING)
        def _(k):
            @pl.when(k < RING - 1)
            def _():
                for part in range(2):
                    ring_copy(d, k, part).wait_send()
                y_copy(d, k, y).wait_send()

            core_copy(d, k, core).wait_send()

        ring_copy(d, last - 1, 2).wait_send()
        y_copy(d, last, y, LAST).wait_send()

    arrive(5, f_of, f_recv)
    result = f_recv[0].astype(jnp.float32)
    for j in range(1, n):
        result = result + f_recv[j].astype(jnp.float32)
    out_ref[...] = result.astype(jnp.bfloat16)
    sent(5, f_of, f_recv)


def fused(hidden, norm_gain, w_query, b_query, w_key, w_value, b_value, w_out, step_ends):
    n = lax.axis_size("tp")
    tok_rows, width = hidden.shape
    block, kv_cols = w_key.shape
    share = w_query.shape[1] // n
    chunk = w_out.shape[1] // n
    bf16, f32 = jnp.bfloat16, jnp.float32
    vmem = pl.BlockSpec(memory_space=pltpu.VMEM)
    far = pl.BlockSpec(memory_space=pl.ANY)
    dma = pltpu.SemaphoreType.DMA
    own_rows = n * (share // HEAD)
    out = pl.pallas_call(
        kernel,
        out_shape=jax.ShapeDtypeStruct((n, chunk), bf16),
        in_specs=[pl.BlockSpec(memory_space=pltpu.SMEM), vmem, vmem, vmem] + [far] * 5,
        out_specs=vmem,
        scratch_shapes=[
            pltpu.VMEM((tok_rows, width), bf16),
            pltpu.VMEM((8, width), f32),
            pltpu.VMEM((2, n, block, kv_cols), bf16),
            pltpu.VMEM((2, tok_rows, kv_cols), f32),
            pltpu.VMEM(w_query.shape, bf16),
            pltpu.VMEM(w_out.shape, bf16),
            pltpu.VMEM((n, 1, block), f32),
            pltpu.VMEM((n, 1, block), f32),
            pltpu.VMEM((n, block), f32),
            pltpu.VMEM((2, n // 2, n, share), f32),
            pltpu.VMEM((n // 2, n, share), f32),
            pltpu.VMEM((n // 2, n, share), f32),
            pltpu.VMEM((2, n // 2, n, share), bf16),
            pltpu.VMEM((n, own_rows, HEAD), bf16),
            pltpu.VMEM((n, own_rows, HEAD), bf16),
            pltpu.VMEM((KV, 8, HEAD), f32),
            pltpu.VMEM((n, 8, HEAD), f32),
            pltpu.VMEM((HEAD, HEAD), f32),
            pltpu.VMEM((HEAD, HEAD), f32),
            pltpu.VMEM((n, n, chunk), f32),
            pltpu.VMEM((n, n, chunk), bf16),
            pltpu.VMEM((n, n, chunk), bf16),
            dma((5,)),
            dma((3, 2, RING)),
            dma((3, 2, RING)),
            dma((2, RING)),
            dma((2, RING)),
            dma((2, RING)),
            dma((2, RING)),
            dma((6, n)),
            dma((6, n)),
            dma((2,)),
            dma((2,)),
        ],
        compiler_params=pltpu.CompilerParams(
            collective_id=0, has_side_effects=True, vmem_limit_bytes=54 * 2**20
        ),
    )(
        step_ends,
        norm_gain.reshape(1, -1),
        b_query.reshape(1, -1),
        b_value.reshape(1, -1),
        hidden,
        w_query,
        w_key,
        w_value,
        w_out,
    )
    return out.reshape(1, n * chunk)


def solution(mesh):
    in_specs = (
        P(("groups", "tp"), None),
        P(),
        P("tp", None),
        P(),
        P("tp", None),
        P("tp", None),
        P(),
        P("tp", None),
        P("groups"),
    )
    out_specs = P(("groups", "tp"), None)
    small = (mesh.shape["groups"], mesh.shape["tp"]) == (2, 16)
    return jax.shard_map(
        fused if small else shards,
        mesh=mesh,
        in_specs=in_specs,
        out_specs=out_specs,
        check_vma=False,
    )
```

```python
import jax
import jax.numpy as jnp
from jax import lax
from jax.experimental import pallas as pl
from jax.experimental.pallas import tpu as pltpu
from jax.sharding import PartitionSpec as P

HEADS = 32
KV = 4
HEAD = 128
MESH = pl.DeviceIdType.MESH


def normed(rows, norm_gain):
    widened = rows.astype(jnp.float32)
    inverse_rms = lax.rsqrt(jnp.mean(widened * widened, axis=-1, keepdims=True) + 1e-06)
    return (widened * inverse_rms * norm_gain).astype(jnp.bfloat16)


def shards(hidden, norm_gain, w_query, b_query, w_key, w_value, b_value, w_out, step_ends):
    devices = lax.axis_size("tp")
    device_index = lax.axis_index("tp")
    tok_rows = hidden.shape[0]
    scored_count = step_ends.shape[0]
    per_owner = scored_count // devices
    group_ratio = HEADS // KV
    normal_rows = normed(hidden, norm_gain)
    key_sum = jnp.dot(
        normal_rows,
        lax.all_gather(w_key, "tp", axis=0, tiled=True),
        preferred_element_type=jnp.float32,
    )
    value_sum = jnp.dot(
        normal_rows,
        lax.all_gather(w_value, "tp", axis=0, tiled=True),
        preferred_element_type=jnp.float32,
    )
    key_rows = key_sum.astype(jnp.bfloat16)
    value_rows = (value_sum + b_value).astype(jnp.bfloat16)
    own_positions = lax.dynamic_slice_in_dim(step_ends, device_index * per_owner, per_owner, 0)
    own_offsets = own_positions - device_index * tok_rows
    own_scored = jnp.take(normal_rows, own_offsets, axis=0)
    scored_cols = lax.all_to_all(own_scored, "tp", split_axis=1, concat_axis=0, tiled=True)
    partial_query = jnp.dot(scored_cols, w_query, preferred_element_type=jnp.float32)
    queries = (lax.psum(partial_query, "tp") + b_query).astype(jnp.bfloat16)
    query_blocks = queries.reshape(scored_count, KV, group_ratio, HEAD)
    key_blocks = key_rows.reshape(tok_rows, KV, HEAD)
    value_blocks = value_rows.reshape(tok_rows, KV, HEAD)
    scores = jnp.einsum(
        "sgrd,tgd->sgrt", query_blocks, key_blocks, preferred_element_type=jnp.float32
    ) * HEAD ** (-0.5)
    key_positions = device_index * tok_rows + jnp.arange(tok_rows, dtype=jnp.int32)
    visible = key_positions[None, None, None, :] <= step_ends[:, None, None, None]
    scores = jnp.where(visible, scores, -1e30)
    local_peak = jnp.max(scores, axis=3)
    global_peak = lax.pmax(local_peak, "tp")
    weights = jnp.where(visible, jnp.exp(scores - global_peak[..., None]), 0.0)
    denominator = jnp.sum(weights, axis=3)
    summed = jnp.einsum(
        "sgrt,tgd->sgrd",
        weights.astype(jnp.bfloat16),
        value_blocks,
        preferred_element_type=jnp.float32,
    )
    owner_sum, owner_total = (
        lax.psum_scatter(
            summed.reshape(scored_count, HEADS * HEAD), "tp", scatter_dimension=0, tiled=True
        ),
        lax.psum_scatter(
            denominator.reshape(scored_count, HEADS), "tp", scatter_dimension=0, tiled=True
        ),
    )
    attended = owner_sum.reshape(per_owner, HEADS, HEAD) / owner_total[..., None]
    mixed_row = attended.reshape(per_owner, HEADS * HEAD).astype(jnp.bfloat16)
    mixed_cols = lax.all_to_all(mixed_row, "tp", split_axis=1, concat_axis=0, tiled=True)
    return lax.psum_scatter(
        jnp.dot(mixed_cols, w_out, preferred_element_type=jnp.float32),
        "tp",
        scatter_dimension=0,
        tiled=True,
    ).astype(jnp.bfloat16)


RING = 8
SPLIT = 176
LAST = 64
NORM_ROWS = 32


def kernel(
    ends_ref, gain_ref, bq_ref, bv_ref, hidden_ref, wq_hbm, wk_hbm, wv_hbm, wo_hbm,
    out_ref,
    normal, own_row, held, acc, wq, wo, row_send, row_recv, cols, pq_send, pq_pair, pq_recv, q_all,
    o_send, o_recv, l_send, l_recv, lmat, tmat, f_rows, f_send, f_recv,
    load_sem, ring_send, ring_recv, y_send, y_recv, core_send, core_recv,
    a2a_send, a2a_recv, pair_send, pair_recv,
):
    n = 16
    me = lax.axis_index("tp")
    y = lax.axis_index("groups")
    core = me % 2
    chip = me // 2
    x = chip % 2
    z = chip // 2
    pos = z * (1 - x) + (RING - 1 - z) * x
    partner = chip * 2 + 1 - core
    block = wk_hbm.shape[0]
    w_hbm = (wk_hbm, wv_hbm)

    def chip_at(p):
        p = (p + 2 * RING) % RING
        far = p // (RING // 2)
        return (1 - far) * (2 * p) + far * (2 * RING - 1 - 2 * p)

    def origin(d, k, c):
        return chip_at(pos + (2 * d - 1) * k) * 2 + c

    late = SPLIT - LAST
    late_rows = pl.ds(pl.multiple_of((1 - y) * (block - late), 16), late)
    early_rows = pl.ds(pl.multiple_of(y * late, 16), block - late)

    def rows_of(part):
        if part == 0:
            return pl.ds(pl.multiple_of(y * (block - SPLIT), 16), SPLIT)
        if part == 1:
            return pl.ds(SPLIT, block - 2 * SPLIT)
        return late_rows

    def ring_part(d, k, part, slot, src):
        return pltpu.make_async_remote_copy(
            src_ref=(held.at[d, slot] if src is None else src).at[rows_of(part)],
            dst_ref=held.at[d, slot, rows_of(part)],
            send_sem=ring_send.at[part, d, k],
            recv_sem=ring_recv.at[part, d, k],
            device_id={"tp": chip_at(pos + (1 - 2 * d)) * 2 + core},
            device_id_type=MESH,
        )

    def ring_copy(d, k, part, src=None):
        return ring_part(d, k, part, origin(d, k, core), src)

    def ring_arrival(d, k, part):
        return ring_part(d, k, part, origin(d, k + 1, core), None)

    def y_copy(d, k, owner, count=SPLIT):
        slot = origin(d, k, core)
        start = (1 - owner) * (SPLIT - count) + owner * (block - SPLIT)
        rows = pl.ds(pl.multiple_of(start, 16), count)
        return pltpu.make_async_remote_copy(
            src_ref=held.at[d, slot, rows],
            dst_ref=held.at[d, slot, rows],
            send_sem=y_send.at[d, k],
            recv_sem=y_recv.at[d, k],
            device_id={"groups": 1 - y},
            device_id_type=MESH,
        )

    def core_rows(d, c, rows, index):
        slot = origin(d, RING - 1, c)
        return pltpu.make_async_remote_copy(
            src_ref=held.at[d, slot, rows],
            dst_ref=held.at[d, slot, rows],
            send_sem=core_send.at[d, index],
            recv_sem=core_recv.at[d, index],
            device_id={"tp": partner},
            device_id_type=MESH,
        )

    def core_copy(d, k, c, src=None):
        slot = origin(d, k, c)
        return pltpu.make_async_remote_copy(
            src_ref=held.at[d, slot] if src is None else src,
            dst_ref=held.at[d, slot],
            send_sem=core_send.at[d, k],
            recv_sem=core_recv.at[d, k],
            device_id={"tp": partner},
            device_id_type=MESH,
        )

    def peer_copy(phase, peer, slot, send, recv):
        return pltpu.make_async_remote_copy(
            src_ref=send,
            dst_ref=recv.at[slot],
            send_sem=a2a_send.at[phase, peer],
            recv_sem=a2a_recv.at[phase, slot],
            device_id={"tp": peer},
            device_id_type=MESH,
        )

    def for_peers(body):
        @pl.loop(1, n)
        def _(k):
            body((me + k) % n)

    def exchange(phase, send_of, recv):
        for_peers(lambda peer: peer_copy(phase, peer, me, send_of(peer), recv).start())

    def arrive(phase, send_of, recv):
        for_peers(lambda peer: peer_copy(phase, peer, peer, send_of(peer), recv).wait_recv())

    def sent(phase, send_of, recv):
        for_peers(lambda peer: peer_copy(phase, peer, me, send_of(peer), recv).wait_send())

    loads = [
        pltpu.make_async_copy(hidden_ref, normal, load_sem.at[0]),
        pltpu.make_async_copy(wq_hbm, wq, load_sem.at[1]),
        pltpu.make_async_copy(wk_hbm, held.at[0, me], load_sem.at[2]),
        pltpu.make_async_copy(wv_hbm, held.at[1, me], load_sem.at[3]),
        pltpu.make_async_copy(wo_hbm, wo, load_sem.at[4]),
    ]
    for load in loads:
        load.start()

    barrier = pltpu.get_barrier_semaphore()
    for_peers(
        lambda peer: pl.semaphore_signal(
            barrier, inc=1, device_id={"tp": peer}, device_id_type=MESH
        )
    )
    pl.semaphore_signal(barrier, inc=1, device_id={"groups": 1 - y}, device_id_type=MESH)
    pl.semaphore_wait(barrier, n)

    for part in range(2):
        for d in range(2):
            ring_copy(d, 0, part, w_hbm[d]).start()
    for d in range(2):
        core_copy(d, 0, core, w_hbm[d]).start()

    row_of = lambda peer: row_send.at[peer]
    tok_rows = normal.shape[0]
    offset = ends_ref[me] % tok_rows
    width = normal.shape[1]
    piece_lanes = 256

    def norm_rows(first, last):
        @pl.loop(first, last)
        def _(i):
            rows = pl.ds(pl.multiple_of(i * NORM_ROWS, NORM_ROWS), NORM_ROWS)
            picked = i * NORM_ROWS + lax.broadcasted_iota(jnp.int32, (NORM_ROWS, 1), 0) == offset
            squares = jnp.zeros((NORM_ROWS, piece_lanes), jnp.float32)
            for c in range(0, width, piece_lanes):
                v = normal[rows, pl.ds(c, piece_lanes)].astype(jnp.float32)
                squares = squares + v * v
            scale = lax.rsqrt(jnp.sum(squares, axis=-1, keepdims=True) / width + 1e-06)
            for c in range(0, width, piece_lanes):
                lanes = pl.ds(c, piece_lanes)
                v = normal[rows, lanes].astype(jnp.float32)
                rounded = (v * scale * gain_ref[:, lanes]).astype(jnp.bfloat16)
                normal[rows, lanes] = rounded
                own = jnp.where(picked, rounded.astype(jnp.float32), 0.0)
                own_row[:, lanes] += own[0:8] + own[8:16] + own[16:24] + own[24:32]

    steps = tok_rows // NORM_ROWS

    def project(k, c):
        @pl.loop(0, 2)
        def _(d):
            slot = origin(d, k, c)
            lanes = pl.ds(pl.multiple_of(slot * block, block), block)
            acc[d] += jnp.dot(
                normal[:, lanes], held[d, slot], preferred_element_type=jnp.float32
            )

    share = wq.shape[1] // n

    def chip_copy(phase, other, slot, send, recv):
        return pltpu.make_async_remote_copy(
            src_ref=send,
            dst_ref=recv.at[slot],
            send_sem=a2a_send.at[phase, other],
            recv_sem=a2a_recv.at[phase, slot],
            device_id={"tp": other * 2 + core},
            device_id_type=MESH,
        )

    def for_chips(body):
        @pl.loop(1, RING)
        def _(k):
            body((chip + k) % RING)

    def pair_copy(phase, send, recv):
        return pltpu.make_async_remote_copy(
            src_ref=send,
            dst_ref=recv,
            send_sem=pair_send.at[phase],
            recv_sem=pair_recv.at[phase],
            device_id={"tp": partner},
            device_id_type=MESH,
        )

    pq_of = lambda other: pq_send.at[core, other]
    q_of = lambda other: q_all.at[core, chip]
    pq_swap = lambda: pair_copy(0, pq_send.at[1 - core], pq_pair)
    q_swap = lambda c: pair_copy(1, q_all.at[c], q_all.at[c])

    @pl.loop(0, RING - 2)
    def _(s):
        for part in range(2):
            for d in range(2):
                ring_arrival(d, s, part).wait_recv()
                ring_copy(d, s + 1, part).start()
                if part == 0:
                    y_copy(d, s + 1, y).start()

        @pl.when(s >= 1)
        def _():
            for d in range(2):
                y_copy(d, s, 1 - y).wait_recv()
                core_copy(d, s, core).start()

        @pl.when(s == 0)
        def _():
            acc[...] = jnp.zeros_like(acc)
            own_row[...] = jnp.zeros_like(own_row)
            for load in loads:
                load.wait()
            norm_rows(0, steps)
            for j in range(n):
                row_send[j] = jnp.sum(own_row[:, pl.ds(j * block, block)], axis=0, keepdims=True)
            row_recv[pl.ds(me, 1)] = row_send[pl.ds(me, 1)]
            exchange(0, row_of, row_recv)
            project(0, core)

        @pl.when(s == 1)
        def _():
            arrive(0, row_of, row_recv)
            for j in range(n):
                cols[j : j + 1, :] = row_recv[j]
            scored = cols[...].astype(jnp.bfloat16)

            @pl.loop(0, n)
            def _(j):
                pq_send[j % 2, j // 2] = jnp.dot(
                    scored,
                    wq[:, pl.ds(pl.multiple_of(j * share, share), share)],
                    preferred_element_type=jnp.float32,
                )

            pq_swap().start()

        @pl.when(s == 2)
        def _():
            pq_swap().wait_recv()
            pq_send[core] = pq_send[core] + pq_pair[...]
            for_chips(lambda other: chip_copy(1, other, chip, pq_of(other), pq_recv).start())
            pq_recv[chip] = pq_send[core, chip]

        @pl.when(s == 3)
        def _():
            for_chips(lambda other: chip_copy(1, other, other, pq_of(other), pq_recv).wait_recv())
            total = pq_recv[0]
            for j in range(1, RING):
                total = total + pq_recv[j]
            bias = bq_ref[:, pl.ds(pl.multiple_of(me * share, share), share)]
            q_all[core, chip] = (total + bias).astype(jnp.bfloat16)
            for_chips(lambda other: chip_copy(2, other, chip, q_of(other), q_all.at[core]).start())

        @pl.when(s == 4)
        def _():
            for_chips(
                lambda other: chip_copy(2, other, other, q_of(other), q_all.at[core]).wait_recv()
            )
            q_swap(core).start()

        @pl.when(s >= 1)
        def _():
            project(s, core)
            for d in range(2):
                core_copy(d, s - 1, 1 - core).wait_recv()
            project(s - 1, 1 - core)

    last = RING - 1
    for d in range(2):
        ring_arrival(d, last - 1, 0).wait_recv()
        y_copy(d, last, y, LAST).start()
    for d in range(2):
        y_copy(d, last - 1, 1 - y).wait_recv()
        ring_copy(d, last - 1, 2).start()
        core_copy(d, last - 1, core).start()
    project(last - 1, core)
    for d in range(2):
        core_copy(d, last - 2, 1 - core).wait_recv()
    project(last - 2, 1 - core)
    for d in range(2):
        ring_arrival(d, last - 1, 1).wait_recv()
        y_copy(d, last, 1 - y, LAST).wait_recv()
        core_rows(d, core, early_rows, last).start()
    for d in range(2):
        ring_arrival(d, last - 1, 2).wait_recv()
        core_rows(d, core, late_rows, last + 1).start()
    for d in range(2):
        core_copy(d, last - 1, 1 - core).wait_recv()
    project(last - 1, 1 - core)
    project(last, core)
    for d in range(2):
        core_rows(d, 1 - core, early_rows, last).wait_recv()
        core_rows(d, 1 - core, late_rows, last + 1).wait_recv()
    project(last, 1 - core)
    q_swap(1 - core).wait_recv()

    key_rows = acc[0].astype(jnp.bfloat16)
    value_rows = (acc[1] + bv_ref[...]).astype(jnp.bfloat16)
    scored_count = n
    group_rows = scored_count * (HEADS // KV)
    per_group = n // KV
    row_of_score = lax.broadcasted_iota(jnp.int32, (group_rows, 1), 0) % scored_count
    limit = jnp.zeros((group_rows, 1), jnp.int32)
    for j in range(scored_count):
        limit = jnp.where(row_of_score == j, ends_ref[j], limit)
    token = lax.broadcasted_iota(jnp.int32, (group_rows, tok_rows), 1) + me * tok_rows
    visible = token <= limit
    own_rows = group_rows // per_group

    for g in range(KV):
        heads = slice(g * HEAD, (g + 1) * HEAD)
        query = jnp.concatenate(
            [
                q_all[(g * per_group + j) % 2, (g * per_group + j) // 2][:, h * HEAD : (h + 1) * HEAD]
                for j in range(per_group)
                for h in range(share // HEAD)
            ],
            axis=0,
        )
        scores = lax.dot_general(
            query,
            key_rows[:, heads],
            (((1,), (1,)), ((), ())),
            preferred_element_type=jnp.float32,
        ) * HEAD ** (-0.5)
        scores = jnp.where(visible, scores, -1e30)
        peak = jnp.max(scores, axis=1, keepdims=True)
        weights = jnp.where(visible, jnp.exp(scores - peak), 0.0)
        total = jnp.sum(weights, axis=1, keepdims=True)
        summed = jnp.dot(
            weights.astype(jnp.bfloat16), value_rows[:, heads], preferred_element_type=jnp.float32
        )
        some = total > 0.0
        total = jnp.where(some, total, 1.0)
        level = jnp.where(some, peak + jnp.log(total), -1e30)
        l_send[g] = jnp.transpose(jnp.broadcast_to(level, (group_rows, HEAD)))[0:1, :]
        part = (summed / total).astype(jnp.bfloat16)
        for j in range(per_group):
            dest = g * per_group + j
            o_send[dest] = part[j * own_rows : (j + 1) * own_rows, :]

            @pl.when(me != dest)
            def _():
                peer_copy(3, dest, me, o_send.at[dest], o_recv).start()
                peer_copy(4, dest, me, l_send.at[g], l_recv).start()

    o_of = lambda peer: o_send.at[peer]
    l_of = lambda peer: l_send.at[peer // per_group]
    o_recv[me] = o_send[me]
    l_recv[me] = l_send[me // per_group]
    arrive(4, l_of, l_recv)
    lmat[...] = jnp.zeros_like(lmat)
    for j in range(n):
        lmat[j : j + 1, :] = l_recv[j]
    levels = lmat[0:n, :]
    mass = jnp.exp(levels - jnp.max(levels, axis=0, keepdims=True))
    lmat[0:n, :] = mass / jnp.sum(mass, axis=0, keepdims=True)
    tmat[...] = jnp.transpose(lmat[...])
    factor = tmat[pl.ds(pl.multiple_of((me % per_group) * own_rows, own_rows), own_rows), :]
    arrive(3, o_of, o_recv)
    attended = jnp.zeros((own_rows, HEAD), jnp.float32)
    for j in range(n):
        attended = attended + factor[:, j : j + 1] * o_recv[j].astype(jnp.float32)
    mixed = jnp.concatenate(
        [attended[0:scored_count], attended[scored_count:own_rows]], axis=1
    ).astype(jnp.bfloat16)

    chunk_lanes = wo.shape[1] // n
    for c in range(n):
        chunk = jnp.dot(
            mixed, wo[:, pl.ds(c * chunk_lanes, chunk_lanes)], preferred_element_type=jnp.float32
        )
        for j in range(n):
            f_rows[j, c : c + 1, :] = chunk[j : j + 1, :]
    f_of = lambda peer: f_send.at[peer]

    @pl.loop(0, n)
    def _(j):
        f_send[j] = f_rows[j].astype(jnp.bfloat16)

    exchange(5, f_of, f_recv)
    f_recv[me] = f_send[me]
    sent(0, row_of, row_recv)
    for_chips(lambda other: chip_copy(1, other, chip, pq_of(other), pq_recv).wait_send())
    for_chips(lambda other: chip_copy(2, other, chip, q_of(other), q_all.at[core]).wait_send())
    pq_swap().wait_send()
    q_swap(core).wait_send()
    sent(3, o_of, o_recv)
    sent(4, l_of, l_recv)
    for d in range(2):
        for part in range(2):
            ring_copy(d, 0, part, w_hbm[d]).wait_send()
        core_copy(d, 0, core, w_hbm[d]).wait_send()

        @pl.loop(1, RING)
        def _(k):
            @pl.when(k < RING - 1)
            def _():
                for part in range(2):
                    ring_copy(d, k, part).wait_send()
                y_copy(d, k, y).wait_send()
                core_copy(d, k, core).wait_send()

        core_rows(d, core, early_rows, last).wait_send()
        core_rows(d, core, late_rows, last + 1).wait_send()
        ring_copy(d, last - 1, 2).wait_send()
        y_copy(d, last, y, LAST).wait_send()

    arrive(5, f_of, f_recv)
    result = f_recv[0].astype(jnp.float32)
    for j in range(1, n):
        result = result + f_recv[j].astype(jnp.float32)
    out_ref[...] = result.astype(jnp.bfloat16)
    sent(5, f_of, f_recv)


def fused(hidden, norm_gain, w_query, b_query, w_key, w_value, b_value, w_out, step_ends):
    n = lax.axis_size("tp")
    tok_rows, width = hidden.shape
    block, kv_cols = w_key.shape
    share = w_query.shape[1] // n
    chunk = w_out.shape[1] // n
    bf16, f32 = jnp.bfloat16, jnp.float32
    vmem = pl.BlockSpec(memory_space=pltpu.VMEM)
    far = pl.BlockSpec(memory_space=pl.ANY)
    dma = pltpu.SemaphoreType.DMA
    own_rows = n * (share // HEAD)
    out = pl.pallas_call(
        kernel,
        out_shape=jax.ShapeDtypeStruct((n, chunk), bf16),
        in_specs=[pl.BlockSpec(memory_space=pltpu.SMEM), vmem, vmem, vmem] + [far] * 5,
        out_specs=vmem,
        scratch_shapes=[
            pltpu.VMEM((tok_rows, width), bf16),
            pltpu.VMEM((8, width), f32),
            pltpu.VMEM((2, n, block, kv_cols), bf16),
            pltpu.VMEM((2, tok_rows, kv_cols), f32),
            pltpu.VMEM(w_query.shape, bf16),
            pltpu.VMEM(w_out.shape, bf16),
            pltpu.VMEM((n, 1, block), f32),
            pltpu.VMEM((n, 1, block), f32),
            pltpu.VMEM((n, block), f32),
            pltpu.VMEM((2, n // 2, n, share), f32),
            pltpu.VMEM((n // 2, n, share), f32),
            pltpu.VMEM((n // 2, n, share), f32),
            pltpu.VMEM((2, n // 2, n, share), bf16),
            pltpu.VMEM((n, own_rows, HEAD), bf16),
            pltpu.VMEM((n, own_rows, HEAD), bf16),
            pltpu.VMEM((KV, 1, HEAD), f32),
            pltpu.VMEM((n, 1, HEAD), f32),
            pltpu.VMEM((HEAD, HEAD), f32),
            pltpu.VMEM((HEAD, HEAD), f32),
            pltpu.VMEM((n, n, chunk), f32),
            pltpu.VMEM((n, n, chunk), bf16),
            pltpu.VMEM((n, n, chunk), bf16),
            dma((5,)),
            dma((3, 2, RING)),
            dma((3, 2, RING)),
            dma((2, RING)),
            dma((2, RING)),
            dma((2, RING + 1)),
            dma((2, RING + 1)),
            dma((6, n)),
            dma((6, n)),
            dma((2,)),
            dma((2,)),
        ],
        compiler_params=pltpu.CompilerParams(
            collective_id=0, has_side_effects=True, vmem_limit_bytes=54 * 2**20
        ),
    )(
        step_ends,
        norm_gain.reshape(1, -1),
        b_query.reshape(1, -1),
        b_value.reshape(1, -1),
        hidden,
        w_query,
        w_key,
        w_value,
        w_out,
    )
    return out.reshape(1, n * chunk)


def solution(mesh):
    in_specs = (
        P(("groups", "tp"), None),
        P(),
        P("tp", None),
        P(),
        P("tp", None),
        P("tp", None),
        P(),
        P("tp", None),
        P("groups"),
    )
    out_specs = P(("groups", "tp"), None)
    small = (mesh.shape["groups"], mesh.shape["tp"]) == (2, 16)
    return jax.shard_map(
        fused if small else shards,
        mesh=mesh,
        in_specs=in_specs,
        out_specs=out_specs,
        check_vma=False,
    )
```
